512 devices in a mesh: tm: 32 (over z, core), pairs: 16 (over y, x).
Axes of the slice: x: 4, y: 4, z: 16, core: 2. Of those that a mesh axis runs over, the one named last changes fastest.
Arguments:
- raw_spectra: bfloat16 [32, 2048, 8192], P('tm', 'pairs'), may hold values from -14 to 14, as said below
- tile_chan: int32 [28, 24], replicated, may hold values from 0 to 2047, as said below
- tile_home: int32 [28], replicated, may hold values from 0 to 15, as said below
- block_home: int32 [16], replicated, may hold values from 0 to 15, each once
Outputs:
- stacks: float32 [16, 512, 512], P('pairs', 'tm')
The draws below stay inside these ranges and needn't reach their ends.
Inputs may be any that keep to these rules, and one draw needn't show every extreme that they name: `raw_spectra`: values lie within the range, with band levels that differ from band to band. `tile_chan`: pairs of a tile are each of its 16 row channels with each of its 8 column channels. All tiles of one device name the same row channels and channels of the same 8 consecutive channel blocks. For each device along pairs, the channels named by its tiles, counted once for each tile that names them, number at most 12 among those held by any one device, and the distinct ones at most 6; both bounds are reached in every draw. `tile_home`: at most 4 tiles belong to one device, and some device owns exactly 4.
All inputs are finite; a program needn't handle non-finite values.
Results may differ from the reference program's by a relative error of at most 0.0059.
Values may be sent and summed in bfloat16 or wider, within the bound.
No kernel may reach another device: no remote copies, remote signals or barrier semaphores. Data moves between devices by JAX's collectives and lax.ppermute only.
A program may use at most 128 MiB of HBM per device.

```python
import math
import jax
import jax.numpy as jnp
from jax import lax

FREQS = 4096
LAGS = 512
BAND = 128
SEG_DEV = 1
CH_DEV = 128
TILE_ROWS = 16
TILE_COLS = 8
TILE_SLOTS = 4
SEGS = 32
CHANNELS = 2048
TILES = 28
N_TM = 32
N_PAIRS = 16


def tile_layout(key):
    key_full = jax.random.fold_in(key, 101)
    key_score = jax.random.fold_in(key, 102)
    key_order = jax.random.fold_in(key, 103)
    key_block = jax.random.fold_in(key, 104)
    key_offset = jax.random.fold_in(key, 105)
    slot_total = N_PAIRS * TILE_SLOTS
    block_span = N_PAIRS // 2
    row_each = TILE_ROWS // block_span
    col_each = TILE_COLS // block_span
    full_device = jax.random.randint(key_full, (), 0, N_PAIRS)
    slot_index = jnp.arange(slot_total, dtype=jnp.int32)
    slot_owner = slot_index // TILE_SLOTS
    slot_score = jax.random.randint(key_score, (slot_total,), 0, 1 << 16) * slot_total + slot_index
    slot_score = jnp.where(slot_index == (N_PAIRS - 1) * TILE_SLOTS, -1, slot_score)
    slot_score = jnp.where(slot_owner == full_device, slot_index - 2 * slot_total, slot_score)
    chosen = jnp.argsort(slot_score)[:TILES]
    chosen = chosen[jax.random.permutation(key_order, TILES)]
    tile_device = (chosen // TILE_SLOTS).astype(jnp.int32)
    onehot = (tile_device[:, None] == jnp.arange(N_PAIRS, dtype=jnp.int32)[None, :]).astype(jnp.int32)
    tile_rank = jnp.sum((jnp.cumsum(onehot, axis=0) - 1) * onehot, axis=1).astype(jnp.int32)
    first_block = jax.random.randint(key_block, (N_PAIRS,), 0, N_PAIRS - block_span + 1)
    first_block = jnp.where(jnp.arange(N_PAIRS, dtype=jnp.int32) == N_PAIRS - 1, N_PAIRS - block_span, first_block)
    order_scores = jax.random.randint(key_offset, (N_PAIRS, block_span, CH_DEV), 0, 1 << 16) * CH_DEV + jnp.arange(CH_DEV, dtype=jnp.int32)
    order_scores = order_scores.at[N_PAIRS - 1, block_span - 1, CH_DEV - 1].set(-1)
    offsets = jnp.argsort(order_scores, axis=2).astype(jnp.int32)
    row_block = jnp.arange(TILE_ROWS, dtype=jnp.int32) // row_each
    row_slot = jnp.arange(TILE_ROWS, dtype=jnp.int32) % row_each
    col_block = jnp.arange(TILE_COLS, dtype=jnp.int32) // col_each
    col_slot = row_each + tile_rank[:, None] * col_each + jnp.arange(TILE_COLS, dtype=jnp.int32)[None, :] % col_each
    row_offset = offsets[tile_device[:, None], row_block[None, :], row_slot[None, :]]
    col_offset = offsets[tile_device[:, None], col_block[None, :], col_slot]
    base_block = first_block[tile_device][:, None]
    row_channel = (base_block + row_block[None, :]) * CH_DEV + row_offset
    col_channel = (base_block + col_block[None, :]) * CH_DEV + col_offset
    return (tile_device, jnp.concatenate([row_channel, col_channel], axis=1).astype(jnp.int32))


def draw_tile_home(key, part):
    tile_device, tile_channels = tile_layout(key)
    return tile_device


def draw_tile_chan(key, part):
    tile_device, tile_channels = tile_layout(key)
    return tile_channels


def draw_raw_spectra(key, part):
    key = jax.random.fold_in(key, 7)
    key_base = jax.random.fold_in(key, 1)
    key_level = jax.random.fold_in(key, 2)
    band_count = FREQS // BAND
    band_level = jax.random.uniform(key_level, (SEGS, CHANNELS, 1, band_count, 1), jnp.float32, -1.2, 1.2)
    base_noise = jnp.clip(jax.random.normal(key_base, (SEGS, CHANNELS, 2, band_count, BAND), jnp.float32), -4.0, 4.0)
    return (base_noise * jnp.exp(band_level)).reshape(SEGS, CHANNELS, 2 * FREQS).astype(jnp.bfloat16)


def setup_inputs(seed: int = 0) -> dict:
    key_of = jax.random.split(jax.random.key(seed), 5)
    raw_spectra = draw_raw_spectra(jax.random.fold_in(key_of[4], 71), 0)
    tile_chan = draw_tile_chan(jax.random.fold_in(key_of[4], 71), 0)
    tile_home = draw_tile_home(jax.random.fold_in(key_of[4], 71), 0)
    block_home = jax.random.permutation(key_of[3], N_PAIRS).astype(jnp.int32)
    return {"raw_spectra": raw_spectra, "tile_chan": tile_chan, "tile_home": tile_home, "block_home": block_home}


def whiten(raw):
    values = raw.astype(jnp.float32)
    half_bins = values.shape[-1] // 2
    banded = values.reshape(values.shape[:-1] + (2, half_bins // BAND, BAND))
    band_power = lax.optimization_barrier(jnp.sum(banded * banded, axis=(-3, -1), keepdims=True)) / BAND
    return (banded * lax.rsqrt(band_power + 1e-06)).reshape(values.shape).astype(jnp.bfloat16)

def make_lags(half_bins, segments):
    bin_index = jnp.arange(half_bins, dtype=jnp.int32)
    lag_index = jnp.arange(LAGS, dtype=jnp.int32) - LAGS // 2
    phase_step = jnp.mod(bin_index[:, None] * lag_index[None, :], 2 * half_bins)
    radians = phase_step.astype(jnp.float32) * (math.pi / half_bins)
    norm_scale = 1.0 / math.sqrt(half_bins * segments)
    return (jnp.concatenate([jnp.cos(radians), -jnp.sin(radians)], axis=0) * norm_scale).astype(jnp.bfloat16)

def slot_table(tile_home, devices, slots):
    onehot = (tile_home[:, None] == jnp.arange(devices, dtype=jnp.int32)[None, :]).astype(jnp.int32)
    tile_rank = lax.optimization_barrier(jnp.sum((jnp.cumsum(onehot, axis=0) - 1) * onehot, axis=1)).astype(jnp.int32)
    slot_match = (tile_home[None, None, :] == jnp.arange(devices, dtype=jnp.int32)[:, None, None]) & (tile_rank[None, None, :] == jnp.arange(slots, dtype=jnp.int32)[None, :, None])
    return slot_match.astype(jnp.int32)

def cross_terms(rows_a, rows_b):
    a_vals = rows_a.astype(jnp.float32)
    b_vals = rows_b.astype(jnp.float32)
    half_bins = a_vals.shape[-1] // 2
    a_real = a_vals[..., :, None, :half_bins]
    a_imag = a_vals[..., :, None, half_bins:]
    b_real = b_vals[..., None, :, :half_bins]
    b_imag = b_vals[..., None, :, half_bins:]
    return jnp.concatenate([a_real * b_real + a_imag * b_imag, a_real * b_imag - a_imag * b_real], axis=-1)

def reference(raw_spectra, tile_chan, tile_home, block_home):
    devices = N_PAIRS
    slot_match = slot_table(tile_home, devices, TILE_SLOTS)
    slot_channels = jnp.einsum('dsk,kr->dsr', slot_match, tile_chan).astype(jnp.int32)
    is_live = (lax.optimization_barrier(jnp.sum(slot_match, axis=2)) > 0).reshape(devices * TILE_SLOTS, 1, 1)
    stored = (block_home[slot_channels // CH_DEV] * CH_DEV + slot_channels % CH_DEV).reshape(-1).astype(jnp.int32)
    grouped = raw_spectra.reshape(N_TM, SEG_DEV, CHANNELS, 2 * FREQS)
    per_tile = TILE_ROWS + TILE_COLS
    zero_stack = jnp.zeros((devices * TILE_SLOTS, TILE_ROWS, TILE_COLS, 2 * FREQS), jnp.float32)

    def segment_term(partial_value, raw_segment):
        picked = whiten(jnp.take(raw_segment, stored, axis=0)).reshape(devices * TILE_SLOTS, per_tile, 2 * FREQS)
        picked = jnp.where(is_live, picked, jnp.zeros((), jnp.bfloat16))
        return (partial_value + cross_terms(picked[:, :TILE_ROWS], picked[:, TILE_ROWS:]), None)

    def group_term(stack_total, raw_group):
        partial_value, _ = lax.scan(segment_term, zero_stack, raw_group)
        rounded = lax.optimization_barrier(partial_value.astype(jnp.bfloat16))
        return (stack_total + rounded.astype(jnp.float32), None)
    stack_total, _ = lax.scan(group_term, zero_stack, grouped)
    lag_table = make_lags(FREQS, SEGS).astype(jnp.float32)
    flat_stack = stack_total.reshape(devices * TILE_SLOTS * TILE_ROWS * TILE_COLS, 2 * FREQS)
    stacks = jnp.dot(flat_stack, lag_table, precision=lax.Precision.HIGHEST, preferred_element_type=jnp.float32)
    return stacks.reshape(devices, TILE_SLOTS * TILE_ROWS * TILE_COLS, LAGS)
```

```python
import functools
import math

import jax
import jax.numpy as jnp
import ml_dtypes
import numpy as np
from jax import lax
from jax.experimental import pallas as pl
from jax.experimental.pallas import tpu as pltpu
from jax.sharding import Mesh
from jax.sharding import PartitionSpec as P

LAGS = 512
BAND = 128
TILE_ROWS = 16
TILE_COLS = 8
TILE_SLOTS = 4
PER_TILE = TILE_ROWS + TILE_COLS
REFS = TILE_SLOTS * PER_TILE
PAIRS = TILE_ROWS * TILE_COLS
CAP = 6
GROUPS = 4
CHUNK = CAP * GROUPS
STEPS = 4
HALF = LAGS // 2
F32 = jnp.float32
BF16 = jnp.bfloat16


def iota(shape, dim):
    return lax.broadcasted_iota(jnp.int32, shape, dim)


def before(size):
    return (iota((size, size), 0) < iota((size, size), 1)).astype(BF16)


def send_kernel(home_ref, block_ref, chan_ref, re_ref, im_ref, out_ref, pick_ref):
    owners = block_ref.shape[0]
    channels = re_ref.shape[1]
    sub = re_ref.shape[2] // GROUPS

    @pl.when(pl.program_id(0) == 0)
    def _():
        me = lax.axis_index("pairs")
        block = jnp.int32(0)
        for b in range(owners):
            block = jnp.where(block_ref[b] == me, b, block)
        chan = chan_ref[...]
        offset = iota((PER_TILE, channels), 1) + block * channels
        owner = iota((owners, channels), 0)
        named = jnp.zeros((owners, channels), F32)
        for t in range(home_ref.shape[0]):
            hit = jnp.max((chan[:, t : t + 1] == offset).astype(F32), axis=0, keepdims=True)
            named = jnp.maximum(named, jnp.where(owner == home_ref[t], hit, 0.0))
        rank = jnp.dot(named.astype(BF16), before(channels), preferred_element_type=F32)
        key = jnp.where(named > 0.0, rank, -1.0)
        row = iota((CHUNK, channels), 0)
        place = (row % CAP).astype(F32)
        group = row // CAP
        parts = []
        for p in range(owners):
            match = jnp.broadcast_to(key[p : p + 1, :], (CHUNK, channels)) == place
            parts.append(
                jnp.concatenate(
                    [jnp.where(match & (group == g), 1.0, 0.0) for g in range(GROUPS)], axis=1
                )
            )
        pick_ref[...] = jnp.concatenate(parts, axis=0).astype(BF16)

    stacked = jnp.concatenate(
        [
            jnp.concatenate(
                [re_ref[0, :, g * sub : (g + 1) * sub], im_ref[0, :, g * sub : (g + 1) * sub]],
                axis=1,
            )
            for g in range(GROUPS)
        ],
        axis=0,
    )
    out_ref[...] = jnp.dot(pick_ref[...], stacked, preferred_element_type=F32).astype(BF16)


def send_rows(raw, chan, tile_home, block_home):
    _, channels, width = raw.shape
    owners = block_home.shape[0]
    wide = width // (2 * STEPS)
    return pl.pallas_call(
        send_kernel,
        grid=(STEPS,),
        in_specs=[
            pl.BlockSpec(memory_space=pltpu.SMEM),
            pl.BlockSpec(memory_space=pltpu.SMEM),
            pl.BlockSpec(chan.shape, lambda i: (0, 0)),
            pl.BlockSpec((1, channels, wide), lambda i: (0, 0, i)),
            pl.BlockSpec((1, channels, wide), lambda i: (0, 0, i + STEPS)),
        ],
        out_specs=pl.BlockSpec((owners * CHUNK, 2 * wide // GROUPS), lambda i: (0, i)),
        out_shape=jax.ShapeDtypeStruct((owners * CHUNK, width // GROUPS), BF16),
        scratch_shapes=[pltpu.VMEM((owners * CHUNK, GROUPS * channels), BF16)],
        compiler_params=pltpu.CompilerParams(vmem_limit_bytes=32 * 1024 * 1024),
        name="send_rows",
    )(tile_home, block_home, chan, raw, raw)


def table_kernel(scale, home_ref, block_ref, chan_ref, lag_ref, place_ref, cos_ref, sin_ref):
    step = pl.program_id(0)
    rows = lag_ref.shape[0]
    low = cos_ref.shape[0]
    high = rows // low
    turn = 2 * rows * STEPS

    def angles(count, first, stride):
        freq = (iota((count, HALF), 0) + first) * stride
        lag = iota((count, HALF), 1) + 1
        return ((freq * lag) & (turn - 1)).astype(F32) * (2.0 * math.pi / turn)

    @pl.when(step == 0)
    def _():
        angle = angles(low, 0, 1)
        cos_ref[...] = jnp.cos(angle)
        sin_ref[...] = jnp.sin(angle)
        me = lax.axis_index("pairs")
        chan = chan_ref[...]
        lane = iota(chan.shape, 1)
        columns = []
        for s in range(TILE_SLOTS):
            tile = jnp.int32(-1)
            seen = jnp.int32(0)
            for t in range(home_ref.shape[0]):
                mine = home_ref[t] == me
                tile = jnp.where(mine & (seen == s), t, tile)
                seen = seen + mine.astype(jnp.int32)
            column = jnp.sum(jnp.where(lane == tile, chan + 1, 0), axis=1, keepdims=True)
            columns.append(column - 1)
        named = jnp.broadcast_to(jnp.concatenate(columns, axis=0), (REFS, BAND))
        cell = iota((REFS, BAND), 1)
        in_block = (named >= 0) & ((named // BAND) == cell)
        at_offset = (named >= 0) & ((named % BAND) == cell)
        block_hot = in_block.astype(F32).astype(BF16)
        offset_hot = at_offset.astype(F32)
        count = lax.dot_general(
            block_hot, offset_hot.astype(BF16), (((0,), (0,)), ((), ())), preferred_element_type=F32
        )
        rank = jnp.dot(
            (count > 0.0).astype(F32).astype(BF16), before(BAND), preferred_element_type=F32
        )
        own_rank = jnp.dot(block_hot, rank.astype(BF16), preferred_element_type=F32)
        position = jnp.sum(own_rank * offset_hot, axis=1, keepdims=True).astype(jnp.int32)
        holder = jnp.zeros((REFS, BAND), jnp.int32)
        for b in range(block_ref.shape[0]):
            holder = jnp.where((named // BAND) == b, block_ref[b], holder)
        place_ref[...] = jnp.where(named >= 0, holder * CHUNK + position, -CHUNK)

    coarse = angles(high, step * high, low)
    cos_high = jnp.cos(coarse) * scale
    sin_high = jnp.sin(coarse) * scale
    cos_low = cos_ref[...]
    sin_low = sin_ref[...]
    for q in range(high):
        ch = cos_high[q : q + 1, :]
        sh = sin_high[q : q + 1, :]
        rows_q = slice(q * low, (q + 1) * low)
        lag_ref[rows_q, :HALF] = (ch * cos_low - sh * sin_low).astype(BF16)
        lag_ref[rows_q, HALF:] = (sh * cos_low + ch * sin_low).astype(BF16)


def tables(bins, segments, chan, tile_home, block_home):
    rows = bins // STEPS
    low = 64
    return pl.pallas_call(
        functools.partial(table_kernel, 1.0 / math.sqrt(bins * segments)),
        grid=(STEPS,),
        in_specs=[
            pl.BlockSpec(memory_space=pltpu.SMEM),
            pl.BlockSpec(memory_space=pltpu.SMEM),
            pl.BlockSpec(chan.shape, lambda i: (0, 0)),
        ],
        out_specs=[
            pl.BlockSpec((rows, LAGS), lambda i: (i, 0)),
            pl.BlockSpec((REFS, BAND), lambda i: (0, 0)),
        ],
        out_shape=[
            jax.ShapeDtypeStruct((bins, LAGS), BF16),
            jax.ShapeDtypeStruct((REFS, BAND), jnp.int32),
        ],
        scratch_shapes=[pltpu.VMEM((low, HALF), F32), pltpu.VMEM((low, HALF), F32)],
        compiler_params=pltpu.CompilerParams(vmem_limit_bytes=32 * 1024 * 1024),
        cost_estimate=pl.CostEstimate(flops=20_000_000, bytes_accessed=8_000_000, transcendentals=0),
        name="tables",
    )(tile_home, block_home, chan)


def stack_kernel(
    zero_scale, place_ref, got_ref, lag_ref, keep_ref, send_ref,
    cross_re, cross_im, even_ref, odd_ref, zero_ref, both_ref,
):
    step = pl.program_id(0)
    sub = got_ref.shape[1] // 2
    received = got_ref.shape[0]

    @pl.when(step == 0)
    def _():
        even_ref[...] = jnp.zeros_like(even_ref)
        odd_ref[...] = jnp.zeros_like(odd_ref)
        zero_ref[...] = jnp.zeros_like(zero_ref)

    white_re, white_im = [], []
    for band in range(sub // BAND):
        re = got_ref[:, band * BAND : (band + 1) * BAND].astype(F32)
        im = got_ref[:, sub + band * BAND : sub + (band + 1) * BAND].astype(F32)
        power = jnp.sum(re * re + im * im, axis=1, keepdims=True) * (1.0 / BAND)
        scale = lax.rsqrt(power + 1e-06)
        white_re.append((re * scale).astype(BF16))
        white_im.append((im * scale).astype(BF16))
    white = jnp.concatenate(white_re + white_im, axis=1)

    place = place_ref[...]
    column = iota((REFS, BAND), 1)
    for g in range(GROUPS):
        chosen = jnp.concatenate(
            [
                jnp.where(column + k * BAND == place + g * CAP, 1.0, 0.0)
                for k in range(received // BAND)
            ],
            axis=1,
        ).astype(BF16)
        rows = jnp.dot(chosen, white, preferred_element_type=F32)
        for s in range(TILE_SLOTS):
            top = s * PER_TILE
            b_re = rows[top + TILE_ROWS : top + PER_TILE, :sub]
            b_im = rows[top + TILE_ROWS : top + PER_TILE, sub:]
            re_parts, im_parts = [], []
            for i in range(TILE_ROWS):
                a_re = rows[top + i : top + i + 1, :sub]
                a_im = rows[top + i : top + i + 1, sub:]
                re_parts.append(a_re * b_re + a_im * b_im)
                im_parts.append(a_re * b_im - a_im * b_re)
            re_all = jnp.concatenate(re_parts, axis=0)
            im_all = jnp.concatenate(im_parts, axis=0)
            span = slice(s * PAIRS, (s + 1) * PAIRS)
            folded = re_all[:, :BAND]
            for band in range(1, sub // BAND):
                folded = folded + re_all[:, band * BAND : (band + 1) * BAND]
            zero_ref[span, :] += folded
            cross_re[span, g * sub : (g + 1) * sub] = re_all.astype(BF16)
            cross_im[span, g * sub : (g + 1) * sub] = im_all.astype(BF16)
    even_ref[...] += jnp.dot(cross_re[...], lag_ref[:, :HALF], preferred_element_type=F32)
    odd_ref[...] += jnp.dot(cross_im[...], lag_ref[:, HALF:], preferred_element_type=F32)

    @pl.when(step == pl.num_programs(0) - 1)
    def _():
        core = lax.axis_index("core")
        even = even_ref[...]
        odd = odd_ref[...]
        at_zero = jnp.sum(zero_ref[...], axis=1, keepdims=True) * zero_scale
        behind = even + odd
        ahead = pltpu.roll(even - odd, 1, 1)
        ahead = jnp.where(iota(ahead.shape, 1) == 0, at_zero, ahead)
        kept = both_ref.shape[2]
        for z in range(both_ref.shape[1]):
            for c in range(2):
                first = (2 * z + c) * kept
                side = jnp.bitwise_xor(core, c)
                both_ref[side, z, :, :HALF] = behind[first : first + kept]
                both_ref[side, z, :, HALF:] = ahead[first : first + kept]
        keep_ref[...] = both_ref[0]
        send_ref[...] = both_ref[1].astype(BF16)


def stack(place, got, lag, depth, segments):
    received, width = got.shape
    bins = lag.shape[0]
    pairs = TILE_SLOTS * PAIRS
    kept = pairs // (2 * depth)
    zero_scale = float(np.float32(1.0 / math.sqrt(bins * segments)).astype(ml_dtypes.bfloat16))
    shape = (depth, kept, LAGS)
    return pl.pallas_call(
        functools.partial(stack_kernel, zero_scale),
        grid=(STEPS,),
        in_specs=[
            pl.BlockSpec((REFS, BAND), lambda i: (0, 0)),
            pl.BlockSpec((received, width // STEPS), lambda i: (0, i)),
            pl.BlockSpec((bins // STEPS, LAGS), lambda i: (i, 0)),
        ],
        out_specs=[
            pl.BlockSpec(shape, lambda i: (0, 0, 0)),
            pl.BlockSpec(shape, lambda i: (0, 0, 0)),
        ],
        out_shape=[jax.ShapeDtypeStruct(shape, F32), jax.ShapeDtypeStruct(shape, BF16)],
        scratch_shapes=[
            pltpu.VMEM((pairs, bins // STEPS), BF16),
            pltpu.VMEM((pairs, bins // STEPS), BF16),
            pltpu.VMEM((pairs, HALF), F32),
            pltpu.VMEM((pairs, HALF), F32),
            pltpu.VMEM((pairs, BAND), F32),
            pltpu.VMEM((2,) + shape, F32),
        ],
        compiler_params=pltpu.CompilerParams(vmem_limit_bytes=48 * 1024 * 1024),
        name="stack",
    )(place, got, lag)


def finish_kernel(parts_ref, out_ref):
    total = parts_ref[0].astype(F32)
    for z in range(1, parts_ref.shape[0]):
        total = total + parts_ref[z].astype(F32)
    mirror = (iota((HALF, HALF), 0) + iota((HALF, HALF), 1) == HALF - 1).astype(F32)
    out_ref[0, :, :HALF] = jnp.dot(
        total[:, :HALF], mirror, precision=lax.Precision.HIGHEST, preferred_element_type=F32
    )
    out_ref[0, :, HALF:] = total[:, HALF:]


def finish(parts):
    _, kept, lags = parts.shape
    return pl.pallas_call(
        finish_kernel,
        out_shape=jax.ShapeDtypeStruct((1, kept, lags), F32),
        name="finish",
    )(parts)


def shards(raw_spectra, tile_chan, tile_home, block_home):
    depth = lax.axis_size("z")
    segments = 2 * depth
    bins = raw_spectra.shape[2] // 2
    chan = tile_chan.T
    outgoing = send_rows(raw_spectra, chan, tile_home, block_home)
    owners = block_home.shape[0]
    incoming = lax.all_to_all(
        outgoing.reshape(owners, CHUNK, -1), "pairs", split_axis=0, concat_axis=0, tiled=True
    )
    lag, place = tables(bins, segments, chan, tile_home, block_home)
    keep, send = stack(place, incoming.reshape(outgoing.shape), lag, depth, segments)
    swapped = lax.ppermute(send, "core", [(0, 1), (1, 0)])
    both = (keep + swapped.astype(F32)).astype(BF16)
    parts = lax.all_to_all(both, "z", split_axis=0, concat_axis=0, tiled=True)
    return finish(parts)


def solution(mesh):
    devices = mesh.devices
    split = Mesh(
        devices.reshape(devices.shape[0] // 2, 2, devices.shape[1]), ("z", "core", "pairs")
    )
    return jax.shard_map(
        shards,
        mesh=split,
        in_specs=(P(("z", "core"), "pairs", None), P(), P(), P()),
        out_specs=P("pairs", ("z", "core"), None),
        check_vma=False,
    )
```

```python
import functools
import math

import jax
import jax.numpy as jnp
import ml_dtypes
import numpy as np
from jax import lax
from jax.experimental import pallas as pl
from jax.experimental.pallas import tpu as pltpu
from jax.sharding import Mesh
from jax.sharding import PartitionSpec as P

LAGS = 512
BAND = 128
TILE_ROWS = 16
TILE_COLS = 8
TILE_SLOTS = 4
PER_TILE = TILE_ROWS + TILE_COLS
REFS = TILE_SLOTS * PER_TILE
PAIRS = TILE_ROWS * TILE_COLS
CAP = 6
GROUPS = 4
CHUNK = CAP * GROUPS
STEPS = 4
SEND_VMEM = 60 * 1024 * 1024
STACK_VMEM = 48 * 1024 * 1024
HALF = LAGS // 2
F32 = jnp.float32
BF16 = jnp.bfloat16


def iota(shape, dim):
    return lax.broadcasted_iota(jnp.int32, shape, dim)


def before(size):
    return (iota((size, size), 0) < iota((size, size), 1)).astype(BF16)


def send_kernel(
    home_in, block_in, chan_in, raw_ref, out_ref,
    rows_ref, sent_ref, home_ref, block_ref, chan_ref, sems, small_sems, out_sems,
):
    owners = block_ref.shape[0]
    _, channels, width = raw_ref.shape
    bins = width // 2
    wide = bins // STEPS
    sub = wide // GROUPS
    copies = []
    for k in range(STEPS):
        for half in range(2):
            lanes = pl.ds(half * bins + k * wide, wide)
            copy = pltpu.make_async_copy(
                raw_ref.at[0, :, lanes], rows_ref.at[:, lanes], sems.at[2 * k + half]
            )
            copies.append(copy)
    small = [
        pltpu.make_async_copy(source, target, small_sems.at[i])
        for i, (source, target) in enumerate(
            ((home_in, home_ref), (block_in, block_ref), (chan_in, chan_ref))
        )
    ]
    for copy in small + copies:
        copy.start()
    for copy in small:
        copy.wait()

    me = lax.axis_index("pairs")
    block = jnp.int32(0)
    for b in range(owners):
        block = jnp.where(block_ref[b] == me, b, block)
    chan = chan_ref[...]
    offset = iota((PER_TILE, channels), 1) + block * channels
    owner = iota((owners, channels), 0)
    named = jnp.zeros((owners, channels), F32)
    for t in range(home_ref.shape[0]):
        hit = jnp.max((chan[:, t : t + 1] == offset).astype(F32), axis=0, keepdims=True)
        named = jnp.maximum(named, jnp.where(owner == home_ref[t], hit, 0.0))
    rank = jnp.dot(named.astype(BF16), before(channels), preferred_element_type=F32)
    key = jnp.where(named > 0.0, rank, -1.0)
    row = iota((CHUNK, channels), 0)
    place = (row % CAP).astype(F32)
    group = row // CAP
    parts = []
    for p in range(owners):
        match = jnp.broadcast_to(key[p : p + 1, :], (CHUNK, channels)) == place
        parts.append(
            jnp.concatenate(
                [jnp.where(match & (group == g), 1.0, 0.0) for g in range(GROUPS)], axis=1
            )
        )
    pick = jnp.concatenate(parts, axis=0).astype(BF16)

    outs = []
    for k in range(STEPS):
        copies[2 * k].wait()
        copies[2 * k + 1].wait()
        stacked = []
        for g in range(GROUPS):
            first = k * wide + g * sub
            stacked.append(
                jnp.concatenate(
                    [rows_ref[:, first : first + sub], rows_ref[:, bins + first : bins + first + sub]],
                    axis=1,
                )
            )
        stacked = jnp.concatenate(stacked, axis=0)
        lanes = slice(2 * k * sub, 2 * (k + 1) * sub)
        sent_ref[:, lanes] = jnp.dot(pick, stacked, preferred_element_type=F32).astype(BF16)
        copy = pltpu.make_async_copy(sent_ref.at[:, lanes], out_ref.at[:, lanes], out_sems.at[k])
        copy.start()
        outs.append(copy)
    for copy in outs:
        copy.wait()


def send_rows(raw, chan, tile_home, block_home):
    _, channels, width = raw.shape
    owners = block_home.shape[0]
    anywhere = pl.BlockSpec(memory_space=pl.ANY)
    shape = (owners * CHUNK, width // GROUPS)
    return pl.pallas_call(
        send_kernel,
        in_specs=[anywhere] * 4,
        out_specs=anywhere,
        out_shape=jax.ShapeDtypeStruct(shape, BF16),
        scratch_shapes=[
            pltpu.VMEM((channels, width), BF16),
            pltpu.VMEM(shape, BF16),
            pltpu.SMEM(tile_home.shape, jnp.int32),
            pltpu.SMEM(block_home.shape, jnp.int32),
            pltpu.VMEM(chan.shape, jnp.int32),
            pltpu.SemaphoreType.DMA((2 * STEPS,)),
            pltpu.SemaphoreType.DMA((3,)),
            pltpu.SemaphoreType.DMA((STEPS,)),
        ],
        compiler_params=pltpu.CompilerParams(vmem_limit_bytes=SEND_VMEM),
        name="send_rows",
    )(tile_home, block_home, chan, raw)


def table_kernel(scale, home_ref, block_ref, chan_ref, lag_ref, place_ref, cos_ref, sin_ref):
    step = pl.program_id(0)
    rows = lag_ref.shape[0]
    low = cos_ref.shape[0]
    high = rows // low
    turn = 2 * rows * STEPS

    def angles(count, first, stride):
        freq = (iota((count, HALF), 0) + first) * stride
        lag = iota((count, HALF), 1) + 1
        return ((freq * lag) & (turn - 1)).astype(F32) * (2.0 * math.pi / turn)

    @pl.when(step == 0)
    def _():
        angle = angles(low, 0, 1)
        cos_ref[...] = jnp.cos(angle)
        sin_ref[...] = jnp.sin(angle)
        me = lax.axis_index("pairs")
        core = lax.axis_index("core")
        chan = chan_ref[...]
        lane = iota(chan.shape, 1)
        columns = []
        for s in range(TILE_SLOTS):
            tile = jnp.int32(-1)
            seen = jnp.int32(0)
            for t in range(home_ref.shape[0]):
                mine = home_ref[t] == me
                tile = jnp.where(mine & (seen == s), t, tile)
                seen = seen + mine.astype(jnp.int32)
            column = jnp.sum(jnp.where(lane == tile, chan + 1, 0), axis=1, keepdims=True) - 1
            sides = [
                jnp.concatenate(
                    [column[i : i + 2] for i in range(2 * c, TILE_ROWS, 4)], axis=0
                )
                for c in range(2)
            ]
            columns.append(jnp.where(core == 0, sides[0], sides[1]))
            columns.append(jnp.where(core == 0, sides[1], sides[0]))
            columns.append(column[TILE_ROWS:])
        named = jnp.broadcast_to(jnp.concatenate(columns, axis=0), (REFS, BAND))
        cell = iota((REFS, BAND), 1)
        in_block = (named >= 0) & ((named // BAND) == cell)
        at_offset = (named >= 0) & ((named % BAND) == cell)
        block_hot = in_block.astype(F32).astype(BF16)
        offset_hot = at_offset.astype(F32)
        count = lax.dot_general(
            block_hot, offset_hot.astype(BF16), (((0,), (0,)), ((), ())), preferred_element_type=F32
        )
        rank = jnp.dot(
            (count > 0.0).astype(F32).astype(BF16), before(BAND), preferred_element_type=F32
        )
        own_rank = jnp.dot(block_hot, rank.astype(BF16), preferred_element_type=F32)
        position = jnp.sum(own_rank * offset_hot, axis=1, keepdims=True).astype(jnp.int32)
        holder = jnp.zeros((REFS, BAND), jnp.int32)
        for b in range(block_ref.shape[0]):
            holder = jnp.where((named // BAND) == b, block_ref[b], holder)
        place_ref[...] = jnp.where(named >= 0, holder * CHUNK + position, -CHUNK)

    coarse = angles(high, step * high, low)
    cos_high = jnp.cos(coarse) * scale
    sin_high = jnp.sin(coarse) * scale
    cos_low = cos_ref[...]
    sin_low = sin_ref[...]
    for q in range(high):
        ch = cos_high[q : q + 1, :]
        sh = sin_high[q : q + 1, :]
        rows_q = slice(q * low, (q + 1) * low)
        lag_ref[rows_q, :HALF] = (ch * cos_low - sh * sin_low).astype(BF16)
        lag_ref[rows_q, HALF:] = (sh * cos_low + ch * sin_low).astype(BF16)


def tables(bins, segments, chan, tile_home, block_home):
    rows = bins // STEPS
    low = 64
    return pl.pallas_call(
        functools.partial(table_kernel, 1.0 / math.sqrt(bins * segments)),
        grid=(STEPS,),
        in_specs=[
            pl.BlockSpec(memory_space=pltpu.SMEM),
            pl.BlockSpec(memory_space=pltpu.SMEM),
            pl.BlockSpec(chan.shape, lambda i: (0, 0)),
        ],
        out_specs=[
            pl.BlockSpec((rows, LAGS), lambda i: (i, 0)),
            pl.BlockSpec((REFS, BAND), lambda i: (0, 0)),
        ],
        out_shape=[
            jax.ShapeDtypeStruct((bins, LAGS), BF16),
            jax.ShapeDtypeStruct((REFS, BAND), jnp.int32),
        ],
        scratch_shapes=[pltpu.VMEM((low, HALF), F32), pltpu.VMEM((low, HALF), F32)],
        compiler_params=pltpu.CompilerParams(vmem_limit_bytes=32 * 1024 * 1024),
        cost_estimate=pl.CostEstimate(flops=20_000_000, bytes_accessed=8_000_000, transcendentals=0),
        name="tables",
    )(tile_home, block_home, chan)


def stack_kernel(
    zero_scale, place_ref, got_ref, lag_ref, keep_ref, send_ref,
    cross_re0, cross_im0, cross_re1, cross_im1, cross_re2, cross_im2, cross_re3, cross_im3, even_ref, odd_ref, zero_ref, chosen_ref,
    table_ref, sems,
):
    received, width = got_ref.shape
    wide = lag_ref.shape[0] // STEPS
    copies = []
    for k in range(STEPS):
        span = pl.ds(k * wide, wide)
        copy = pltpu.make_async_copy(lag_ref.at[span], table_ref.at[span], sems.at[k])
        copy.start()
        copies.append(copy)
    sub = wide // GROUPS
    crosses = [
        (cross_re0, cross_im0), (cross_re1, cross_im1), (cross_re2, cross_im2), (cross_re3, cross_im3)
    ]

    place = place_ref[...]
    column = iota((REFS, BAND), 1)
    for g in range(GROUPS):
        chosen_ref[g * REFS : (g + 1) * REFS, :] = jnp.concatenate(
            [
                jnp.where(column + k * BAND == place + g * CAP, 1.0, 0.0)
                for k in range(received // BAND)
            ],
            axis=1,
        ).astype(BF16)

    def multiply(k, half):
        total, lanes = ((even_ref, slice(0, HALF)), (odd_ref, slice(HALF, LAGS)))[half]
        product = jnp.dot(
            crosses[k][half][...],
            table_ref[k * wide : (k + 1) * wide, lanes],
            preferred_element_type=F32,
        )
        total[...] = product if k == 0 else total[...] + product

    for k in range(STEPS):
        if k == 2:
            for copy in copies:
                copy.wait()
        white_re, white_im = [], []
        for band in range(sub // BAND):
            first = 2 * k * sub + band * BAND
            re = got_ref[:, first : first + BAND].astype(F32)
            im = got_ref[:, first + sub : first + sub + BAND].astype(F32)
            power = jnp.sum(re * re + im * im, axis=1, keepdims=True) * (1.0 / BAND)
            scale = lax.rsqrt(power + 1e-06)
            white_re.append((re * scale).astype(BF16))
            white_im.append((im * scale).astype(BF16))
        white = jnp.concatenate(white_re + white_im, axis=1)
        rows = jnp.dot(chosen_ref[...], white, preferred_element_type=F32)
        cross_re, cross_im = crosses[k]
        for g in range(GROUPS):
            for s in range(TILE_SLOTS):
                top = g * REFS + s * PER_TILE
                b_re = rows[top + TILE_ROWS : top + PER_TILE, :sub]
                b_im = rows[top + TILE_ROWS : top + PER_TILE, sub:]
                for side in range(2):
                    re_parts, im_parts = [], []
                    for i in range(side * TILE_ROWS // 2, (side + 1) * TILE_ROWS // 2):
                        a_re = rows[top + i : top + i + 1, :sub]
                        a_im = rows[top + i : top + i + 1, sub:]
                        re_parts.append(a_re * b_re + a_im * b_im)
                        im_parts.append(a_re * b_im - a_im * b_re)
                    re_all = jnp.concatenate(re_parts, axis=0)
                    im_all = jnp.concatenate(im_parts, axis=0)
                    first = (side * TILE_SLOTS + s) * PAIRS // 2
                    span = slice(first, first + PAIRS // 2)
                    folded = re_all[:, :BAND]
                    for band in range(1, sub // BAND):
                        folded = folded + re_all[:, band * BAND : (band + 1) * BAND]
                    zero_ref[span, :] = folded if k + g == 0 else zero_ref[span, :] + folded
                    cross_re[span, g * sub : (g + 1) * sub] = re_all.astype(BF16)
                    cross_im[span, g * sub : (g + 1) * sub] = im_all.astype(BF16)
            if k == 2:
                multiply(g // 2, g % 2)
            if k == 3 and g % 2 == 1:
                multiply(2, g // 2)
    multiply(STEPS - 1, 0)
    multiply(STEPS - 1, 1)

    mirror = (iota((HALF, HALF), 0) + iota((HALF, HALF), 1) == HALF - 1).astype(F32).astype(BF16)
    rows_each = even_ref.shape[0] // 2
    for side, out_ref in enumerate((keep_ref, send_ref)):
        span = slice(side * rows_each, (side + 1) * rows_each)
        even = even_ref[span, :]
        odd = odd_ref[span, :]
        behind = even + odd
        high = behind.astype(BF16)
        mirrored = jnp.dot(high, mirror, preferred_element_type=F32)
        if side == 0:
            low = (behind - high.astype(F32)).astype(BF16)
            mirrored = mirrored + jnp.dot(low, mirror, preferred_element_type=F32)
        ahead = pltpu.roll(even - odd, 1, 1)
        at_zero = jnp.sum(zero_ref[span, :], axis=1, keepdims=True) * zero_scale
        ahead = jnp.where(iota(ahead.shape, 1) == 0, at_zero, ahead)
        out_ref[:, :HALF] = mirrored.astype(out_ref.dtype)
        out_ref[:, HALF:] = ahead.astype(out_ref.dtype)


def stack(place, got, lag, segments):
    received, _ = got.shape
    bins = lag.shape[0]
    pairs = TILE_SLOTS * PAIRS
    zero_scale = float(np.float32(1.0 / math.sqrt(bins * segments)).astype(ml_dtypes.bfloat16))
    shape = (pairs // 2, LAGS)
    vmem = pl.BlockSpec(memory_space=pltpu.VMEM)
    return pl.pallas_call(
        functools.partial(stack_kernel, zero_scale),
        in_specs=[vmem, vmem, pl.BlockSpec(memory_space=pl.ANY)],
        out_specs=[vmem] * 2,
        out_shape=[jax.ShapeDtypeStruct(shape, F32), jax.ShapeDtypeStruct(shape, BF16)],
        scratch_shapes=[pltpu.VMEM((pairs, bins // STEPS), BF16)] * (2 * STEPS)
        + [
            pltpu.VMEM((pairs, HALF), F32),
            pltpu.VMEM((pairs, HALF), F32),
            pltpu.VMEM((pairs, BAND), F32),
            pltpu.VMEM((GROUPS * REFS, received), BF16),
            pltpu.VMEM(lag.shape, BF16),
            pltpu.SemaphoreType.DMA((STEPS,)),
        ],
        compiler_params=pltpu.CompilerParams(vmem_limit_bytes=STACK_VMEM),
        name="stack",
    )(place, got, lag)


def shards(raw_spectra, tile_chan, tile_home, block_home):
    depth = lax.axis_size("z")
    segments = 2 * depth
    bins = raw_spectra.shape[2] // 2
    chan = tile_chan.T
    outgoing = send_rows(raw_spectra, chan, tile_home, block_home)
    owners = block_home.shape[0]
    incoming = lax.all_to_all(
        outgoing.reshape(owners, CHUNK, -1), "pairs", split_axis=0, concat_axis=0, tiled=True
    )
    lag, place = tables(bins, segments, chan, tile_home, block_home)
    keep, send = stack(place, incoming.reshape(outgoing.shape), lag, segments)
    swapped = lax.ppermute(send, "core", [(0, 1), (1, 0)])
    both = (keep + swapped.astype(F32)).astype(BF16).reshape(depth, -1, LAGS)
    parts = lax.all_to_all(both, "z", split_axis=0, concat_axis=0, tiled=True)
    return jnp.sum(parts.astype(F32), axis=0)[None]


def solution(mesh):
    devices = mesh.devices
    split = Mesh(
        devices.reshape(devices.shape[0] // 2, 2, devices.shape[1]), ("z", "core", "pairs")
    )
    return jax.shard_map(
        shards,
        mesh=split,
        in_specs=(P(("z", "core"), "pairs", None), P(), P(), P()),
        out_specs=P("pairs", ("z", "core"), None),
        check_vma=False,
    )
```
